256 devices in a mesh: rows: 32 (over z, x), width: 8 (over y, core).
Axes of the slice: x: 4, y: 4, z: 8, core: 2. Of those that a mesh axis runs over, the one named last changes fastest.
Arguments:
- slab: bfloat16 [262144, 5120], P('rows', 'width'), may hold values from -200 to 200
- basis: bfloat16 [5120, 256], P('width'), may hold values from -3 to 3
Outputs:
- projected: float32 [5120, 256], P('width', 'rows')
- triangle: float32 [256, 256], replicated
The draws below stay inside these ranges and needn't reach their ends.
All inputs are finite; a program needn't handle non-finite values.
Results may differ from the reference program's by a relative error of at most 0.00047.
Values may be sent and summed in bfloat16 or wider, within the bound.
No kernel may reach another device: no remote copies, remote signals or barrier semaphores. Data moves between devices by JAX's collectives and lax.ppermute only.
A program may use at most 128 MiB of HBM per device.

```python
import math
import jax
import jax.numpy as jnp
from jax import lax

D = 5120
K = 256
ROWS = 262144


def draw_slab(key, part):
    key = jax.random.fold_in(key, 11)
    first, second, third = jax.random.split(key, 3)
    row_scale = jnp.exp(jax.random.uniform(second, (ROWS, 1), jnp.float32, math.log(0.3), math.log(3.0)))
    col_scale = jnp.exp(jax.random.uniform(third, (1, D), jnp.float32, math.log(0.3), math.log(3.0)))
    place = jnp.arange(ROWS, dtype=jnp.float32).reshape(ROWS, 1) / ROWS
    rising = jnp.exp(math.log(3.0) * place)
    base = jnp.clip(jax.random.normal(first, (ROWS, D), jnp.float32), -6.0, 6.0)
    return (base * row_scale * rising * col_scale).astype(jnp.bfloat16)


def draw_basis(key, part):
    key = jax.random.fold_in(key, 23)
    first, second = jax.random.split(key, 2)
    col_scale = jnp.exp(jax.random.uniform(second, (1, K), jnp.float32, math.log(0.3), math.log(3.0)))
    base = jnp.clip(jax.random.normal(first, (D, K), jnp.float32), -6.0, 6.0)
    return (base * col_scale / math.sqrt(D)).astype(jnp.bfloat16)


def setup_inputs(seed: int = 0) -> dict:
    key_list = jax.random.split(jax.random.key(seed), 3)
    slab = draw_slab(jax.random.fold_in(key_list[2], 71), 0)
    basis = draw_basis(jax.random.fold_in(key_list[2], 71), 0)
    return {"slab": slab, "basis": basis}


def gram_of(left):
    return jnp.einsum('rk,rj->kj', left, left, precision=lax.Precision.HIGHEST)

def reference(slab, basis):
    sketch = jnp.dot(slab.astype(jnp.float32), basis.astype(jnp.float32), preferred_element_type=jnp.float32)
    lower = jnp.linalg.cholesky(gram_of(sketch))
    ortho = lax.linalg.triangular_solve(lower, sketch, left_side=False, lower=True, transpose_a=True)
    ortho_half = ortho.astype(jnp.bfloat16)
    projected = lax.dot_general(slab.astype(jnp.float32), ortho_half.astype(jnp.float32), (((0,), (0,)), ((), ())), preferred_element_type=jnp.float32)
    return (projected, lower.T / jnp.sqrt(jnp.float32(ROWS)))
```

```python
import functools
import jax
import jax.numpy as jnp
from jax import lax
from jax.experimental import pallas as pl
from jax.experimental.pallas import tpu as pltpu
from jax.sharding import PartitionSpec as P

f32 = jnp.float32
HI = lax.Precision.HIGHEST


def factor_diagonal(block, b, g=8):
    lane = lax.broadcasted_iota(jnp.int32, (b, 128), 1)
    row = lax.broadcasted_iota(jnp.int32, (b, 128), 0)
    a = jnp.concatenate([block, jnp.zeros((b, 128 - b), f32)], axis=1)
    a = jnp.where(lane == row + b, 1.0, a)
    sub = lax.broadcasted_iota(jnp.int32, (8, 128), 0)
    done = []
    for s in range(0, b, g):
        top, rest = a[0:g, :], a[g:, :]
        tiles = (b - s - g) // 8
        rows = [jnp.broadcast_to(top[k : k + 1, :], (8, 128)) for k in range(g)]
        u = {
            (k, m): jnp.broadcast_to(top[k : k + 1, s + m : s + m + 1], (8, 128))
            for k in range(g)
            for m in range(k, g)
        }
        cols = [
            [
                jnp.broadcast_to(rest[8 * t : 8 * t + 8, s + k : s + k + 1], (8, 128))
                for t in range(tiles)
            ]
            for k in range(g)
        ]
        for k in range(g):
            scale = lax.rsqrt(u[k, k])
            rows[k] = rows[k] * scale
            cols[k] = [c * scale for c in cols[k]]
            for m in range(k + 1, g):
                u[k, m] = u[k, m] * scale
            for m in range(k + 1, g):
                for q in range(m, g):
                    u[m, q] = u[m, q] - u[k, m] * u[k, q]
                rows[m] = rows[m] - u[k, m] * rows[k]
                cols[m] = [c - u[k, m] * d for c, d in zip(cols[m], cols[k])]
        final = rows[0]
        for k in range(1, g):
            final = jnp.where(sub == k, rows[k], final)
        done.append(final)
        if tiles:
            out = []
            for t in range(tiles):
                v = rest[8 * t : 8 * t + 8, :]
                for k in range(g):
                    v = v - cols[k][t] * rows[k]
                out.append(v)
            a = jnp.concatenate(out, axis=0)
    return jnp.concatenate(done, axis=0)[:, b : 2 * b]


def factor_kernel(b, n, g_ref, r_ref, inv_ref, m_ref):
    m_ref[:, 0:n] = g_ref[...]
    ri = lax.broadcasted_iota(jnp.int32, (n, n), 0)
    ci = lax.broadcasted_iota(jnp.int32, (n, n), 1)
    m_ref[:, n : 2 * n] = jnp.where(ri == ci, 1.0, 0.0)
    for s in range(0, n, b):
        inverse = factor_diagonal(m_ref[s : s + b, s : s + b], b)
        rows = jnp.dot(
            inverse, m_ref[s : s + b, :], precision=HI, preferred_element_type=f32
        )
        rr = lax.broadcasted_iota(jnp.int32, (b, n), 0)
        cc = lax.broadcasted_iota(jnp.int32, (b, n), 1)
        left = jnp.where(cc >= rr + s, rows[:, 0:n], 0.0)
        right = rows[:, n : 2 * n]
        r_ref[s : s + b, :] = left
        inv_ref[s : s + b, :] = right
        if s + b < n:
            update = lax.dot_general(
                left,
                jnp.concatenate([left, right], axis=1),
                (((0,), (0,)), ((), ())),
                precision=HI,
                preferred_element_type=f32,
            )
            m_ref[s + b : n, :] = m_ref[s + b : n, :] - update[s + b : n, :]


def factor_and_inverse(gram, b=64):
    n = gram.shape[0]
    vmem = pl.BlockSpec(memory_space=pltpu.VMEM)
    return pl.pallas_call(
        functools.partial(factor_kernel, b, n),
        out_shape=(jax.ShapeDtypeStruct((n, n), f32),) * 2,
        in_specs=[vmem],
        out_specs=(vmem, vmem),
        scratch_shapes=[pltpu.VMEM((n, 2 * n), f32)],
        cost_estimate=pl.CostEstimate(
            flops=12 * n**3, bytes_accessed=12 * n * n, transcendentals=n
        ),
    )(gram)


def shift_core(x):
    return lax.ppermute(x, "width", [(i, i ^ 1) for i in range(8)])


def shift_y(x, k):
    return lax.ppermute(x, "width", [(i, (i + 2 * k) % 8) for i in range(8)])


def shift_x(x, k):
    return lax.ppermute(
        x, "rows", [(i, i // 4 * 4 + (i % 4 + k) % 4) for i in range(32)]
    )


def shift_z(x, k):
    return lax.ppermute(x, "rows", [(i, (i + 4 * k) % 32) for i in range(32)])


def sum_of_four(x, shift):
    return (x + shift(x, 2)) + (shift(x, 1) + shift(x, -1))


def sum_of_eight(x, shift):
    even = (x + shift(x, 4)) + (shift(x, 2) + shift(x, -2))
    odd = (shift(x, 1) + shift(x, -3)) + (shift(x, 3) + shift(x, -1))
    return even + odd


def sum_everywhere(x):
    core = lax.axis_index("width") % 2
    half = x.shape[0] // 2
    own = lax.dynamic_slice_in_dim(x, core * half, half, 0)
    other = lax.dynamic_slice_in_dim(x, (1 - core) * half, half, 0)
    own = own + shift_core(other)
    own = sum_of_four(own, shift_y)
    own = sum_of_four(own, shift_x)
    own = sum_of_eight(own, shift_z)
    other = shift_core(own)
    first = jnp.where(core == 0, own, other)
    second = jnp.where(core == 0, other, own)
    return jnp.concatenate([first, second], axis=0)


def shards(slab, basis):
    total_rows = slab.shape[0] * lax.axis_size("rows")
    partial_sketch = jnp.dot(slab, basis, preferred_element_type=f32)
    sketch = lax.psum_scatter(partial_sketch, "width", scatter_dimension=0, tiled=True)
    whole = lax.all_gather(sketch.astype(jnp.bfloat16), "width", axis=0, tiled=True)
    gram = lax.dot_general(
        sketch, sketch, (((0,), (0,)), ((), ())), precision=HI, preferred_element_type=f32
    )
    gram = sum_everywhere(gram)
    factor, inverse = factor_and_inverse(gram)
    value = lax.dot_general(
        whole, slab, (((0,), (0,)), ((), ())), preferred_element_type=f32
    )
    value = jnp.dot(inverse, value, precision=HI, preferred_element_type=f32)
    pieces = lax.all_to_all(value, "rows", 0, 0, tiled=True)
    projected = jnp.sum(pieces.reshape(32, 8, -1), axis=0).T
    triangle = factor / jnp.sqrt(f32(total_rows))
    return (projected, triangle)


def solution(mesh):
    return jax.shard_map(
        shards,
        mesh=mesh,
        in_specs=(P("rows", "width"), P("width", None)),
        out_specs=(P("width", "rows"), P()),
        check_vma=False,
    )
```

```python
import functools
import jax
import jax.numpy as jnp
from jax import lax
from jax.experimental import pallas as pl
from jax.experimental.pallas import tpu as pltpu
from jax.sharding import PartitionSpec as P

f32 = jnp.float32
f16 = jnp.float16
HI = lax.Precision.HIGHEST


def factor_diagonal(block, b, g=8):
    lane = lax.broadcasted_iota(jnp.int32, (b, 128), 1)
    row = lax.broadcasted_iota(jnp.int32, (b, 128), 0)
    a = jnp.concatenate([block, jnp.zeros((b, 128 - b), f32)], axis=1)
    a = jnp.where(lane == row + b, 1.0, a)
    sub = lax.broadcasted_iota(jnp.int32, (8, 128), 0)
    done = []
    for s in range(0, b, g):
        top, rest = a[0:g, :], a[g:, :]
        tiles = (b - s - g) // 8
        rows = [jnp.broadcast_to(top[k : k + 1, :], (8, 128)) for k in range(g)]
        u = {
            (k, m): jnp.broadcast_to(top[k : k + 1, s + m : s + m + 1], (8, 128))
            for k in range(g)
            for m in range(k, g)
        }
        cols = [
            [
                jnp.broadcast_to(rest[8 * t : 8 * t + 8, s + k : s + k + 1], (8, 128))
                for t in range(tiles)
            ]
            for k in range(g)
        ]
        for k in range(g):
            scale = lax.rsqrt(u[k, k])
            rows[k] = rows[k] * scale
            cols[k] = [c * scale for c in cols[k]]
            for m in range(k + 1, g):
                u[k, m] = u[k, m] * scale
            for m in range(k + 1, g):
                for q in range(m, g):
                    u[m, q] = u[m, q] - u[k, m] * u[k, q]
                rows[m] = rows[m] - u[k, m] * rows[k]
                cols[m] = [c - u[k, m] * d for c, d in zip(cols[m], cols[k])]
        final = rows[0]
        for k in range(1, g):
            final = jnp.where(sub == k, rows[k], final)
        done.append(final)
        if tiles:
            out = []
            for t in range(tiles):
                v = rest[8 * t : 8 * t + 8, :]
                for k in range(g):
                    v = v - cols[k][t] * rows[k]
                out.append(v)
            a = jnp.concatenate(out, axis=0)
    return jnp.concatenate(done, axis=0)[:, b : 2 * b]


def factor_kernel(
    b, n, g_ref, sketch_ref, slab_ref, t_ref, p_ref, m_ref, y_ref, s_ref, x_ref, sems
):
    count, _, rows = sketch_ref.shape
    copies = []
    for i in range(count):
        held = pl.ds(i * rows, rows)
        copies.append(
            (
                pltpu.make_async_copy(sketch_ref.at[i], s_ref.at[i], sems.at[0, i]),
                pltpu.make_async_copy(slab_ref.at[held], x_ref.at[held], sems.at[1, i]),
            )
        )
        for copy in copies[-1]:
            copy.start()
    m_ref[:, 0:n] = g_ref[...]
    ri = lax.broadcasted_iota(jnp.int32, (n, n), 0)
    ci = lax.broadcasted_iota(jnp.int32, (n, n), 1)
    m_ref[:, n : 2 * n] = jnp.where(ri == ci, 1.0, 0.0)
    steps = n // b
    for s in range(0, n, b):
        mine = range(s // b * count // steps, (s // b + 1) * count // steps)
        for i in mine:
            for copy in copies[i]:
                copy.wait()
        value = None if s == 0 else y_ref[...]
        for i in mine:
            term = jnp.dot(
                s_ref[i], x_ref[i * rows : (i + 1) * rows, :], preferred_element_type=f32
            )
            value = term if value is None else value + term
        y_ref[...] = value
        inverse = factor_diagonal(m_ref[s : s + b, s : s + b], b)
        rows_now = jnp.dot(
            inverse, m_ref[s : s + b, :], precision=HI, preferred_element_type=f32
        )
        rr = lax.broadcasted_iota(jnp.int32, (b, n), 0)
        cc = lax.broadcasted_iota(jnp.int32, (b, n), 1)
        left = jnp.where(cc >= rr + s, rows_now[:, 0:n], 0.0)
        right = rows_now[:, n : 2 * n]
        t_ref[s : s + b, :] = left
        if s + b < n:
            update = lax.dot_general(
                left,
                jnp.concatenate([left, right], axis=1),
                (((0,), (0,)), ((), ())),
                precision=HI,
                preferred_element_type=f32,
            )
            m_ref[s + b : n, :] = m_ref[s + b : n, :] - update[s + b : n, :]
        m_ref[s : s + b, n : 2 * n] = right
    value = jnp.dot(
        m_ref[:, n : 2 * n], y_ref[...], precision=HI, preferred_element_type=f32
    )
    d = value.shape[1]
    value, e = coded(value)
    p_ref[:, 0:d] = value
    p_ref[:, d : d + 128] = jnp.broadcast_to(e, (n, 128))


def factor_and_project(gram, sketch, slab, b=64):
    n = gram.shape[0]
    rows, d = slab.shape
    vmem = pl.BlockSpec(memory_space=pltpu.VMEM)
    far = pl.BlockSpec(memory_space=pl.ANY)
    return pl.pallas_call(
        functools.partial(factor_kernel, b, n),
        out_shape=(
            jax.ShapeDtypeStruct((n, n), f32),
            jax.ShapeDtypeStruct((n, d + 128), f32),
        ),
        in_specs=[vmem, far, far],
        out_specs=(vmem, vmem),
        scratch_shapes=[
            pltpu.VMEM((n, 2 * n), f32),
            pltpu.VMEM((n, d), f32),
            pltpu.VMEM(sketch.shape, sketch.dtype),
            pltpu.VMEM((rows, d), slab.dtype),
            pltpu.SemaphoreType.DMA((2, sketch.shape[0])),
        ],
        compiler_params=pltpu.CompilerParams(vmem_limit_bytes=40 << 20),
        cost_estimate=pl.CostEstimate(
            flops=12 * n**3 + 2 * rows * n * d,
            bytes_accessed=12 * n * n + 2 * rows * (n + d),
            transcendentals=n,
        ),
    )(
        gram,
        pltpu.with_memory_space_constraint(sketch, pltpu.HBM),
        pltpu.with_memory_space_constraint(slab, pltpu.HBM),
    )


ROWS_AT_ONCE = 512
VMEM_LIMIT = 24 << 20


def coded(x):
    e = jnp.ceil(jnp.log2(jnp.maximum(jnp.max(jnp.abs(x), keepdims=True), 1e-30)))
    return x * jnp.exp2(14.0 - e), e


def write_coded(out_ref, x):
    n = x.shape[0]
    y, e = coded(x)
    out_ref[0:n, :] = y
    out_ref[n : n + 16, :] = jnp.broadcast_to(e, (16, x.shape[1]))


def read_coded(ref):
    n = ref.shape[0] - 16
    return ref[0:n, :] * jnp.exp2(ref[n : n + 1, :] - 14.0)


FAR = ((2, 0), (2, 1))
NEAR = ((1, 1), (3, 0), (1, 0), (3, 1))
HERE = ((0, 0), (0, 1))


def piece(ring, core, s, h):
    start = (((ring + s) % 4 * 2 + core) * 2 + h) * ROWS_AT_ONCE
    return pl.ds(pl.multiple_of(start, ROWS_AT_ONCE), ROWS_AT_ONCE)


def load_kernel(
    place_ref, slab_ref, basis_ref, held_ref, held_basis_ref, first_ref, here_ref, sems
):
    ring, core = place_ref[0], place_ref[1]
    pieces = [(c, s, h) for c in (1 - core, core) for s, h in FAR + NEAR + HERE]
    copies = [pltpu.make_async_copy(basis_ref, held_basis_ref, sems.at[len(pieces)])]
    copies[0].start()
    for i, (c, s, h) in enumerate(pieces):
        rows = piece(ring, c, s, h)
        copies.append(pltpu.make_async_copy(slab_ref.at[rows], held_ref.at[rows], sems.at[i]))
        copies[-1].start()
    copies.pop(0).wait()
    size = ROWS_AT_ONCE + 16
    outs = [first_ref.at[i * size : (i + 1) * size] for i in range(len(FAR + NEAR))]
    outs += [here_ref.at[i * size : (i + 1) * size] for i in range(len(HERE))]
    for i in range(0, len(outs), 2):
        for copy in copies[i : i + 2]:
            copy.wait()
        for out, (c, s, h) in zip(outs[i : i + 2], pieces[i : i + 2]):
            x = jnp.dot(
                held_ref[piece(ring, c, s, h), :],
                held_basis_ref[...],
                preferred_element_type=f32,
            )
            write_coded(out, x)
    for copy in copies[len(outs) :]:
        copy.wait()


def load_and_sketch(slab, basis, place):
    rows, d = slab.shape
    k, size = basis.shape[1], ROWS_AT_ONCE + 16
    vmem = pl.BlockSpec(memory_space=pltpu.VMEM)
    far = pl.BlockSpec(memory_space=pl.ANY)
    return pl.pallas_call(
        load_kernel,
        out_shape=(
            pltpu.VMEM((rows, d), slab.dtype),
            pltpu.VMEM((d, k), basis.dtype),
            jax.ShapeDtypeStruct((len(FAR + NEAR) * size, k), f32),
            jax.ShapeDtypeStruct((len(HERE) * size, k), f32),
        ),
        in_specs=[pl.BlockSpec(memory_space=pltpu.SMEM), far, far],
        out_specs=(vmem,) * 4,
        scratch_shapes=[pltpu.SemaphoreType.DMA((17,))],
        compiler_params=pltpu.CompilerParams(vmem_limit_bytes=VMEM_LIMIT),
        cost_estimate=pl.CostEstimate(
            flops=rows * d * k, bytes_accessed=2 * rows * (d + 2 * k), transcendentals=0
        ),
    )(
        place,
        pltpu.with_memory_space_constraint(slab, pltpu.HBM),
        pltpu.with_memory_space_constraint(basis, pltpu.HBM),
    )


def sketch_kernel(pieces, place_ref, slab_ref, basis_ref, other_ref, *outs):
    ring, core = place_ref[0], place_ref[1]
    b = ROWS_AT_ONCE
    for i, ((s, h), out) in enumerate(zip(pieces, outs)):
        x = jnp.dot(
            slab_ref[piece(ring, core, s, h), :], basis_ref[...], preferred_element_type=f32
        )
        x = x + read_coded(other_ref.at[i * (b + 16) : (i + 1) * (b + 16)])
        if out.shape[0] == b:
            out[...] = x
        else:
            write_coded(out, x)


def sketch_rows(held, basis, place, other, pieces, plain):
    b, (d, k) = ROWS_AT_ONCE, basis.shape
    count = len(pieces)
    vmem = pl.BlockSpec(memory_space=pltpu.VMEM)
    return pl.pallas_call(
        functools.partial(sketch_kernel, pieces),
        out_shape=[
            jax.ShapeDtypeStruct((b + 16 if i < count - plain else b, k), f32)
            for i in range(count)
        ],
        in_specs=[pl.BlockSpec(memory_space=pltpu.SMEM), vmem, vmem, vmem],
        out_specs=[vmem] * count,
        compiler_params=pltpu.CompilerParams(vmem_limit_bytes=VMEM_LIMIT),
        cost_estimate=pl.CostEstimate(
            flops=2 * count * b * d * k,
            bytes_accessed=count * b * (2 * d + 8 * k),
            transcendentals=0,
        ),
    )(
        place,
        pltpu.with_memory_space_constraint(held, pltpu.VMEM),
        pltpu.with_memory_space_constraint(basis, pltpu.VMEM),
        other,
    )


def add_kernel(a_ref, b_ref, c_ref, d_ref, up_ref, down_ref):
    write_coded(up_ref, a_ref[...] + read_coded(b_ref))
    write_coded(down_ref, c_ref[...] + read_coded(d_ref))


def add_received(a, b, c, d):
    vmem = pl.BlockSpec(memory_space=pltpu.VMEM)
    return pl.pallas_call(
        add_kernel,
        out_shape=(jax.ShapeDtypeStruct(b.shape, f32),) * 2,
        in_specs=[vmem] * 4,
        out_specs=(vmem, vmem),
        compiler_params=pltpu.CompilerParams(vmem_limit_bytes=VMEM_LIMIT),
        cost_estimate=pl.CostEstimate(
            flops=4 * a.size, bytes_accessed=24 * a.size, transcendentals=0
        ),
    )(a, b, c, d)


def gram_kernel(a_ref, b_ref, c_ref, d_ref, e_ref, f_ref, gram_ref, half_ref):
    n = gram_ref.shape[0]
    total = None
    b = a_ref.shape[0]
    for i, (own, first, second) in enumerate(
        ((a_ref, b_ref, c_ref), (d_ref, e_ref, f_ref))
    ):
        s = (own[...] + read_coded(first) + read_coded(second)).T
        top = s.astype(jnp.bfloat16)
        rest = (s - top.astype(f32)).astype(jnp.bfloat16)
        half_ref[:, i * b : (i + 1) * b] = top
        both = jnp.concatenate([top, rest], axis=0)
        g = lax.dot_general(
            both, both, (((1,), (1,)), ((), ())), preferred_element_type=f32
        )
        g = (g[0:n, 0:n] + g[n:, n:]) + (g[0:n, n:] + g[n:, 0:n])
        total = g if total is None else total + g
    gram_ref[...] = total


def gram_and_half(low, high):
    rows, k = low[0].shape
    vmem = pl.BlockSpec(memory_space=pltpu.VMEM)
    return pl.pallas_call(
        gram_kernel,
        out_shape=(
            jax.ShapeDtypeStruct((k, k), f32),
            jax.ShapeDtypeStruct((k, 2 * rows), jnp.bfloat16),
        ),
        in_specs=[vmem] * 6,
        out_specs=(vmem, vmem),
        compiler_params=pltpu.CompilerParams(vmem_limit_bytes=VMEM_LIMIT),
        cost_estimate=pl.CostEstimate(
            flops=16 * rows * k * k, bytes_accessed=28 * rows * k, transcendentals=0
        ),
    )(*low, *high)


def shift_core(x):
    return lax.ppermute(x, "width", [(i, i ^ 1) for i in range(8)])


def shift_y(x, k):
    return lax.ppermute(x, "width", [(i, (i + 2 * k) % 8) for i in range(8)])


def shift_x(x, k):
    return lax.ppermute(
        x, "rows", [(i, i // 4 * 4 + (i % 4 + k) % 4) for i in range(32)]
    )


def shift_z(x, k):
    return lax.ppermute(x, "rows", [(i, (i + 4 * k) % 32) for i in range(32)])


def sum_of_four(x, shift, step=1):
    return (x + shift(x, 2 * step)) + (shift(x, step) + shift(x, -step))


def block_of(x, index, size):
    return lax.dynamic_slice_in_dim(x, index * size, size, 0)


def sum_everywhere(x):
    core = lax.axis_index("width") % 2
    col = lax.axis_index("rows") % 4
    plane = lax.axis_index("rows") // 4
    half, piece = x.shape[0] // 2, x.shape[0] // 8
    own = block_of(x, core, half) + shift_core(block_of(x, 1 - core, half))
    parts = [block_of(own, (col + k) % 4, piece) for k in range(4)]
    own = (parts[0] + shift_x(parts[2], 2)) + (
        shift_x(parts[1], 1) + shift_x(parts[3], -1)
    )
    own = sum_of_four(own, shift_z, 2)
    own = own + lax.ppermute(own, "rows", [(i, i ^ 4) for i in range(32)])
    own = sum_of_four(own, shift_y)
    ring = [own, shift_x(own, -1), shift_x(own, 2), shift_x(own, 1)]
    ring = jnp.concatenate(ring + ring, axis=0)
    own = lax.dynamic_slice_in_dim(ring, (4 - col) % 4 * piece, half, 0)
    other = shift_core(own)
    first = jnp.where(core == 0, own, other)
    second = jnp.where(core == 0, other, own)
    return jnp.concatenate([first, second], axis=0)


def shards(slab, basis):
    width = lax.axis_index("width")
    total_rows = slab.shape[0] * lax.axis_size("rows")
    place = jnp.stack([width // 2, width % 2]).astype(jnp.int32)

    held, held_basis, first, here = load_and_sketch(slab, basis, place)
    first = shift_core(first.astype(f16))
    first, here = lax.optimization_barrier((first, here))
    here = shift_core(here.astype(f16))
    first = sketch_rows(held, held_basis, place, first.astype(f32), FAR + NEAR, 2)
    far_up, far_down, near_up, near_down, up, down = first
    far_up, far_down = shift_y(far_up.astype(f16), 1), shift_y(far_down.astype(f16), -1)
    near_up = shift_y(near_up.astype(f16), 1)
    near_down = shift_y(near_down.astype(f16), -1)
    low, high = sketch_rows(held, held_basis, place, here.astype(f32), HERE, 2)

    up, down = add_received(up, far_up.astype(f32), down, far_down.astype(f32))
    up, down = shift_y(up.astype(f16), 1), shift_y(down.astype(f16), -1)
    gram, sketch = gram_and_half(
        (low, up.astype(f32), near_down.astype(f32)),
        (high, near_up.astype(f32), down.astype(f32)),
    )

    sketch = lax.all_gather(sketch, "width", axis=0)
    factor, value = factor_and_project(sum_everywhere(gram), sketch, slab)
    pieces = lax.all_to_all(value.astype(f16), "rows", 0, 0, tiled=True).reshape(32, 8, -1)
    n = slab.shape[1]
    scale = jnp.exp2(pieces[:, :, n : n + 1].astype(f32) - 14.0)
    projected = jnp.sum(pieces[:, :, :n].astype(f32) * scale, axis=0).T
    triangle = factor / jnp.sqrt(f32(total_rows))
    return (projected, triangle)


def solution(mesh):
    return jax.shard_map(
        shards,
        mesh=mesh,
        in_specs=(P("rows", "width"), P("width", None)),
        out_specs=(P("width", "rows"), P()),
        check_vma=False,
    )
```

```python
import functools
import jax
import jax.numpy as jnp
from jax import lax
from jax.experimental import pallas as pl
from jax.experimental.pallas import tpu as pltpu
from jax.sharding import PartitionSpec as P

f32 = jnp.float32
f16 = jnp.float16
HI = lax.Precision.HIGHEST


def factor_diagonal(block, b, g=8):
    lane = lax.broadcasted_iota(jnp.int32, (b, 128), 1)
    row = lax.broadcasted_iota(jnp.int32, (b, 128), 0)
    a = jnp.concatenate([block, jnp.zeros((b, 128 - b), f32)], axis=1)
    a = jnp.where(lane == row + b, 1.0, a)
    sub = lax.broadcasted_iota(jnp.int32, (8, 128), 0)
    done = []
    for s in range(0, b, g):
        top, rest = a[0:g, :], a[g:, :]
        tiles = (b - s - g) // 8
        rows = [jnp.broadcast_to(top[k : k + 1, :], (8, 128)) for k in range(g)]
        u = {
            (k, m): jnp.broadcast_to(top[k : k + 1, s + m : s + m + 1], (8, 128))
            for k in range(g)
            for m in range(k, g)
        }
        cols = [
            [
                jnp.broadcast_to(rest[8 * t : 8 * t + 8, s + k : s + k + 1], (8, 128))
                for t in range(tiles)
            ]
            for k in range(g)
        ]
        for k in range(g):
            scale = lax.rsqrt(u[k, k])
            rows[k] = rows[k] * scale
            cols[k] = [c * scale for c in cols[k]]
            for m in range(k + 1, g):
                u[k, m] = u[k, m] * scale
            for m in range(k + 1, g):
                for q in range(m, g):
                    u[m, q] = u[m, q] - u[k, m] * u[k, q]
                rows[m] = rows[m] - u[k, m] * rows[k]
                cols[m] = [c - u[k, m] * d for c, d in zip(cols[m], cols[k])]
        final = rows[0]
        for k in range(1, g):
            final = jnp.where(sub == k, rows[k], final)
        done.append(final)
        if tiles:
            out = []
            for t in range(tiles):
                v = rest[8 * t : 8 * t + 8, :]
                for k in range(g):
                    v = v - cols[k][t] * rows[k]
                out.append(v)
            a = jnp.concatenate(out, axis=0)
    return jnp.concatenate(done, axis=0)[:, b : 2 * b]


ROWS_AT_ONCE = 512
VMEM_LIMIT = 24 << 20


def coded(x):
    e = jnp.ceil(jnp.log2(jnp.maximum(jnp.max(jnp.abs(x), keepdims=True), 1e-30)))
    return x * jnp.exp2(14.0 - e), e


def write_coded(out_ref, x):
    n = x.shape[0]
    y, e = coded(x)
    out_ref[0:n, :] = y
    out_ref[n : n + 16, :] = jnp.broadcast_to(e, (16, x.shape[1]))


def read_coded(ref):
    n = ref.shape[0] - 16
    return ref[0:n, :] * jnp.exp2(ref[n : n + 1, :] - 14.0)


FIRST = ((2, 0), (2, 1), (1, 1), (3, 0))
SECOND = ((1, 0), (3, 1), (0, 0), (0, 1))


def piece(ring, core, s, h):
    start = (((ring + s) % 4 * 2 + core) * 2 + h) * ROWS_AT_ONCE
    return pl.ds(pl.multiple_of(start, ROWS_AT_ONCE), ROWS_AT_ONCE)


def load_kernel(
    place_ref, slab_ref, basis_ref, held_ref, held_basis_ref, first_ref, second_ref, sems
):
    ring, core = place_ref[0], place_ref[1]
    pieces = [(c, s, h) for c in (1 - core, core) for s, h in FIRST + SECOND]
    copies = [pltpu.make_async_copy(basis_ref, held_basis_ref, sems.at[len(pieces)])]
    copies[0].start()
    for i, (c, s, h) in enumerate(pieces):
        rows = piece(ring, c, s, h)
        copies.append(pltpu.make_async_copy(slab_ref.at[rows], held_ref.at[rows], sems.at[i]))
        copies[-1].start()
    copies.pop(0).wait()
    size = ROWS_AT_ONCE + 16
    outs = [first_ref.at[i * size : (i + 1) * size] for i in range(len(FIRST))]
    outs += [second_ref.at[i * size : (i + 1) * size] for i in range(len(SECOND))]
    for i in range(0, len(outs), 2):
        for copy in copies[i : i + 2]:
            copy.wait()
        for out, (c, s, h) in zip(outs[i : i + 2], pieces[i : i + 2]):
            x = jnp.dot(
                held_ref[piece(ring, c, s, h), :],
                held_basis_ref[...],
                preferred_element_type=f32,
            )
            write_coded(out, x)
    for copy in copies[len(outs) :]:
        copy.wait()


def load_and_sketch(slab, basis, place):
    rows, d = slab.shape
    k, size = basis.shape[1], ROWS_AT_ONCE + 16
    vmem = pl.BlockSpec(memory_space=pltpu.VMEM)
    far = pl.BlockSpec(memory_space=pl.ANY)
    return pl.pallas_call(
        load_kernel,
        out_shape=(
            pltpu.VMEM((rows, d), slab.dtype),
            pltpu.VMEM((d, k), basis.dtype),
            jax.ShapeDtypeStruct((len(FIRST) * size, k), f32),
            jax.ShapeDtypeStruct((len(SECOND) * size, k), f32),
        ),
        in_specs=[pl.BlockSpec(memory_space=pltpu.SMEM), far, far],
        out_specs=(vmem,) * 4,
        scratch_shapes=[pltpu.SemaphoreType.DMA((17,))],
        compiler_params=pltpu.CompilerParams(vmem_limit_bytes=VMEM_LIMIT),
        cost_estimate=pl.CostEstimate(
            flops=rows * d * k, bytes_accessed=2 * rows * (d + 2 * k), transcendentals=0
        ),
    )(
        place,
        pltpu.with_memory_space_constraint(slab, pltpu.HBM),
        pltpu.with_memory_space_constraint(basis, pltpu.HBM),
    )


def sketch_kernel(pieces, place_ref, slab_ref, basis_ref, other_ref, *outs):
    ring, core = place_ref[0], place_ref[1]
    b = ROWS_AT_ONCE
    for i, ((s, h), out) in enumerate(zip(pieces, outs)):
        x = jnp.dot(
            slab_ref[piece(ring, core, s, h), :], basis_ref[...], preferred_element_type=f32
        )
        x = x + read_coded(other_ref.at[i * (b + 16) : (i + 1) * (b + 16)])
        if out.shape[0] == b:
            out[...] = x
        else:
            write_coded(out, x)


def sketch_rows(held, basis, place, other, pieces, plain):
    b, (d, k) = ROWS_AT_ONCE, basis.shape
    count = len(pieces)
    vmem = pl.BlockSpec(memory_space=pltpu.VMEM)
    return pl.pallas_call(
        functools.partial(sketch_kernel, pieces),
        out_shape=[
            jax.ShapeDtypeStruct((b + 16 if i < count - plain else b, k), f32)
            for i in range(count)
        ],
        in_specs=[pl.BlockSpec(memory_space=pltpu.SMEM), vmem, vmem, vmem],
        out_specs=[vmem] * count,
        compiler_params=pltpu.CompilerParams(vmem_limit_bytes=VMEM_LIMIT),
        cost_estimate=pl.CostEstimate(
            flops=2 * count * b * d * k,
            bytes_accessed=count * b * (2 * d + 8 * k),
            transcendentals=0,
        ),
    )(
        place,
        pltpu.with_memory_space_constraint(held, pltpu.VMEM),
        pltpu.with_memory_space_constraint(basis, pltpu.VMEM),
        other,
    )


def add_kernel(a_ref, b_ref, c_ref, d_ref, up_ref, down_ref):
    write_coded(up_ref, a_ref[...] + read_coded(b_ref))
    write_coded(down_ref, c_ref[...] + read_coded(d_ref))


def add_received(a, b, c, d):
    vmem = pl.BlockSpec(memory_space=pltpu.VMEM)
    return pl.pallas_call(
        add_kernel,
        out_shape=(jax.ShapeDtypeStruct(b.shape, f32),) * 2,
        in_specs=[vmem] * 4,
        out_specs=(vmem, vmem),
        compiler_params=pltpu.CompilerParams(vmem_limit_bytes=VMEM_LIMIT),
        cost_estimate=pl.CostEstimate(
            flops=4 * a.size, bytes_accessed=24 * a.size, transcendentals=0
        ),
    )(a, b, c, d)


def gram_kernel(a_ref, b_ref, c_ref, d_ref, e_ref, f_ref, gram_ref, half_ref):
    n = gram_ref.shape[0]
    total = None
    for i, (own, first, second) in enumerate(
        ((a_ref, b_ref, c_ref), (d_ref, e_ref, f_ref))
    ):
        s = (own[...] + read_coded(first) + read_coded(second)).T
        top = s.astype(jnp.bfloat16)
        rest = (s - top.astype(f32)).astype(jnp.bfloat16)
        half_ref[i] = top
        both = jnp.concatenate([top, rest], axis=0)
        g = lax.dot_general(
            both, both, (((1,), (1,)), ((), ())), preferred_element_type=f32
        )
        g = (g[0:n, 0:n] + g[n:, n:]) + (g[0:n, n:] + g[n:, 0:n])
        total = g if total is None else total + g
    gram_ref[...] = total


def gram_and_half(low, high):
    rows, k = low[0].shape
    vmem = pl.BlockSpec(memory_space=pltpu.VMEM)
    return pl.pallas_call(
        gram_kernel,
        out_shape=(
            jax.ShapeDtypeStruct((k, k), f32),
            jax.ShapeDtypeStruct((2, k, rows), jnp.bfloat16),
        ),
        in_specs=[vmem] * 6,
        out_specs=(vmem, vmem),
        compiler_params=pltpu.CompilerParams(vmem_limit_bytes=VMEM_LIMIT),
        cost_estimate=pl.CostEstimate(
            flops=16 * rows * k * k, bytes_accessed=28 * rows * k, transcendentals=0
        ),
    )(*low, *high)


def factor_kernel(b, n, total_rows, place_ref, slab_ref, *refs):
    parts, halves, refs = refs[:2], refs[2:12], refs[12:]
    t_ref, p_ref, m_ref, y_ref, x_ref, sems = refs
    ring, core = place_ref[0], place_ref[1]
    sketch = []
    for c, (own, up, down, low, high) in ((core, halves[:5]), (1 - core, halves[5:])):
        for s, ref in ((0, own), (3, up), (1, down)):
            sketch += [(s, c, 0, ref.at[0]), (s, c, 1, ref.at[1])]
        sketch += [(2, c, 0, low), (2, c, 1, high)]
    count, rows = len(sketch), ROWS_AT_ONCE
    copies = []
    for i, (s, c, h, _) in enumerate(sketch):
        copies.append(
            pltpu.make_async_copy(slab_ref.at[piece(ring, c, s, h)], x_ref.at[i], sems.at[i])
        )
        copies[-1].start()
    size = n // 8
    for c, ref in zip((core, 1 - core), parts):
        for i in range(4):
            start = (c * 4 + (place_ref[2] + i) % 4) * size
            m_ref[pl.ds(pl.multiple_of(start, size), size), 0:n] = ref[
                i * size : (i + 1) * size, :
            ]
    ri = lax.broadcasted_iota(jnp.int32, (n, n), 0)
    ci = lax.broadcasted_iota(jnp.int32, (n, n), 1)
    m_ref[:, n : 2 * n] = jnp.where(ri == ci, 1.0, 0.0)
    steps = n // b
    for s in range(0, n, b):
        mine = range(s // b * count // steps, (s // b + 1) * count // steps)
        for i in mine:
            copies[i].wait()
        value = None if s == 0 else y_ref[...]
        for i in mine:
            term = jnp.dot(sketch[i][3][...], x_ref[i], preferred_element_type=f32)
            value = term if value is None else value + term
        y_ref[...] = value
        inverse = factor_diagonal(m_ref[s : s + b, s : s + b], b)
        rows_now = jnp.dot(
            inverse, m_ref[s : s + b, :], precision=HI, preferred_element_type=f32
        )
        rr = lax.broadcasted_iota(jnp.int32, (b, n), 0)
        cc = lax.broadcasted_iota(jnp.int32, (b, n), 1)
        left = jnp.where(cc >= rr + s, rows_now[:, 0:n], 0.0)
        right = rows_now[:, n : 2 * n]
        t_ref[s : s + b, :] = left / jnp.sqrt(f32(total_rows))
        if s + b < n:
            update = lax.dot_general(
                left,
                jnp.concatenate([left, right], axis=1),
                (((0,), (0,)), ((), ())),
                precision=HI,
                preferred_element_type=f32,
            )
            m_ref[s + b : n, :] = m_ref[s + b : n, :] - update[s + b : n, :]
        m_ref[s : s + b, n : 2 * n] = right
    value = jnp.dot(
        m_ref[:, n : 2 * n], y_ref[...], precision=HI, preferred_element_type=f32
    )
    d = value.shape[1]
    value, e = coded(value)
    p_ref[:, 0:d] = value
    p_ref[:, d : d + 128] = jnp.broadcast_to(e, (n, 128))


def factor_and_project(gram, halves, slab, place, total_rows, b=64):
    n = gram[0].shape[1]
    rows, d = slab.shape
    count = rows // ROWS_AT_ONCE
    vmem = pl.BlockSpec(memory_space=pltpu.VMEM)
    return pl.pallas_call(
        functools.partial(factor_kernel, b, n, total_rows),
        out_shape=(
            jax.ShapeDtypeStruct((n, n), f32),
            jax.ShapeDtypeStruct((n, d + 128), f32),
        ),
        in_specs=[
            pl.BlockSpec(memory_space=pltpu.SMEM),
            pl.BlockSpec(memory_space=pl.ANY),
            *[vmem] * (len(gram) + len(halves)),
        ],
        out_specs=(vmem, vmem),
        scratch_shapes=[
            pltpu.VMEM((n, 2 * n), f32),
            pltpu.VMEM((n, d), f32),
            pltpu.VMEM((count, ROWS_AT_ONCE, d), slab.dtype),
            pltpu.SemaphoreType.DMA((count,)),
        ],
        compiler_params=pltpu.CompilerParams(vmem_limit_bytes=VMEM_LIMIT),
        cost_estimate=pl.CostEstimate(
            flops=12 * n**3 + 2 * rows * n * d,
            bytes_accessed=12 * n * n + 2 * rows * (n + d),
            transcendentals=n,
        ),
    )(place, pltpu.with_memory_space_constraint(slab, pltpu.HBM), *gram, *halves)


def shift_core(x):
    return lax.ppermute(x, "width", [(i, i ^ 1) for i in range(8)])


def shift_y(x, k):
    return lax.ppermute(x, "width", [(i, (i + 2 * k) % 8) for i in range(8)])


def shift_x(x, k):
    return lax.ppermute(
        x, "rows", [(i, i // 4 * 4 + (i % 4 + k) % 4) for i in range(32)]
    )


def shift_z(x, k):
    return lax.ppermute(x, "rows", [(i, (i + 4 * k) % 32) for i in range(32)])


def sum_of_four(x, shift, step=1):
    return (x + shift(x, 2 * step)) + (shift(x, step) + shift(x, -step))


def block_of(x, index, size):
    return lax.dynamic_slice_in_dim(x, index * size, size, 0)


def sum_everywhere(x, beside):
    core = lax.axis_index("width") % 2
    col = lax.axis_index("rows") % 4
    half, piece = x.shape[0] // 2, x.shape[0] // 8
    own = block_of(x, core, half) + shift_core(block_of(x, 1 - core, half))
    parts = [block_of(own, (col + k) % 4, piece) for k in range(4)]
    own = (parts[0] + shift_x(parts[2], 2)) + (
        shift_x(parts[1], 1) + shift_x(parts[3], -1)
    )
    own = sum_of_four(own, shift_z, 2)
    own, first = lax.optimization_barrier((own, beside(0, None)))
    own = own + lax.ppermute(own, "rows", [(i, i ^ 4) for i in range(32)])
    own = sum_of_four(own, shift_y)
    own, second = lax.optimization_barrier((own, beside(1, first)))
    ring = [own, shift_x(own, -1), shift_x(own, 2), shift_x(own, 1)]
    own = jnp.concatenate(ring, axis=0)
    return (own, shift_core(own)), first + second


def shards(slab, basis):
    width = lax.axis_index("width")
    total_rows = slab.shape[0] * lax.axis_size("rows")
    place = jnp.stack([width // 2, width % 2, lax.axis_index("rows") % 4]).astype(jnp.int32)

    held, held_basis, first, second = load_and_sketch(slab, basis, place)
    first = shift_core(first.astype(f16))
    first, second = lax.optimization_barrier((first, second))
    second = shift_core(second.astype(f16))
    far_up, far_down, near_up, near_down = sketch_rows(
        held, held_basis, place, first.astype(f32), FIRST, 0
    )
    far_up, far_down = shift_y(far_up.astype(f16), 1), shift_y(far_down.astype(f16), -1)
    near_up = shift_y(near_up.astype(f16), 1)
    near_down = shift_y(near_down.astype(f16), -1)
    up, down, low, high = sketch_rows(
        held, held_basis, place, second.astype(f32), SECOND, 4
    )

    up, down = add_received(up, far_up.astype(f32), down, far_down.astype(f32))
    up, down = shift_y(up.astype(f16), 1), shift_y(down.astype(f16), -1)
    gram, sketch = gram_and_half(
        (low, up.astype(f32), near_down.astype(f32)),
        (high, near_up.astype(f32), down.astype(f32)),
    )

    def gather(step, got):
        if step == 0:
            return (shift_y(sketch, 1), shift_y(sketch, -1))
        return (shift_y(got[0][0], 1), shift_y(got[1][1], -1))

    gram, others = sum_everywhere(gram, gather)
    halves = (sketch, *others)
    halves += tuple(shift_core(x) for x in halves)
    triangle, value = factor_and_project(gram, halves, slab, place, total_rows)
    pieces = lax.all_to_all(value.astype(f16), "rows", 0, 0, tiled=True).reshape(32, 8, -1)
    n = slab.shape[1]
    scale = jnp.exp2(pieces[:, :, n : n + 1].astype(f32) - 14.0)
    projected = jnp.sum(pieces[:, :, :n].astype(f32) * scale, axis=0).T
    return (projected, triangle)


def solution(mesh):
    return jax.shard_map(
        shards,
        mesh=mesh,
        in_specs=(P("rows", "width"), P("width", None)),
        out_specs=(P("width", "rows"), P()),
        check_vma=False,
    )
```

```python
import functools
import jax
import jax.numpy as jnp
from jax import lax
from jax.experimental import pallas as pl
from jax.experimental.pallas import tpu as pltpu
from jax.sharding import PartitionSpec as P

f32 = jnp.float32
f16 = jnp.float16
HI = lax.Precision.HIGHEST


def factor_diagonal(block, b, g=8):
    lane = lax.broadcasted_iota(jnp.int32, (b, 128), 1)
    row = lax.broadcasted_iota(jnp.int32, (b, 128), 0)
    a = jnp.concatenate([block, jnp.zeros((b, 128 - b), f32)], axis=1)
    a = jnp.where(lane == row + b, 1.0, a)
    sub = lax.broadcasted_iota(jnp.int32, (8, 128), 0)
    done = []
    for s in range(0, b, g):
        top, rest = a[0:g, :], a[g:, :]
        tiles = (b - s - g) // 8
        rows = [jnp.broadcast_to(top[k : k + 1, :], (8, 128)) for k in range(g)]
        u = {
            (k, m): jnp.broadcast_to(top[k : k + 1, s + m : s + m + 1], (8, 128))
            for k in range(g)
            for m in range(k, g)
        }
        cols = [
            [
                jnp.broadcast_to(rest[8 * t : 8 * t + 8, s + k : s + k + 1], (8, 128))
                for t in range(tiles)
            ]
            for k in range(g)
        ]
        for k in range(g):
            scale = lax.rsqrt(u[k, k])
            rows[k] = rows[k] * scale
            cols[k] = [c * scale for c in cols[k]]
            for m in range(k + 1, g):
                u[k, m] = u[k, m] * scale
            for m in range(k + 1, g):
                for q in range(m, g):
                    u[m, q] = u[m, q] - u[k, m] * u[k, q]
                rows[m] = rows[m] - u[k, m] * rows[k]
                cols[m] = [c - u[k, m] * d for c, d in zip(cols[m], cols[k])]
        final = rows[0]
        for k in range(1, g):
            final = jnp.where(sub == k, rows[k], final)
        done.append(final)
        if tiles:
            out = []
            for t in range(tiles):
                v = rest[8 * t : 8 * t + 8, :]
                for k in range(g):
                    v = v - cols[k][t] * rows[k]
                out.append(v)
            a = jnp.concatenate(out, axis=0)
    return jnp.concatenate(done, axis=0)[:, b : 2 * b]


ROWS_AT_ONCE = 512
VMEM_LIMIT = 24 << 20


def coded(x):
    e = jnp.ceil(jnp.log2(jnp.maximum(jnp.max(jnp.abs(x), keepdims=True), 1e-30)))
    return x * jnp.exp2(14.0 - e), e


def write_coded(out_ref, x):
    n = x.shape[0]
    y, e = coded(x)
    out_ref[0:n, :] = y
    out_ref[n : n + 16, :] = jnp.broadcast_to(e, (16, x.shape[1]))


def read_coded(ref):
    n = ref.shape[0] - 16
    return ref[0:n, :] * jnp.exp2(ref[n : n + 1, :] - 14.0)


FIRST = ((2, 0), (2, 1), (1, 1), (3, 0))
SECOND = ((1, 0), (3, 1), (0, 0), (0, 1))


def piece(ring, core, s, h):
    start = (((ring + s) % 4 * 2 + core) * 2 + h) * ROWS_AT_ONCE
    return pl.ds(pl.multiple_of(start, ROWS_AT_ONCE), ROWS_AT_ONCE)


def load_kernel(pieces, place_ref, slab_ref, basis_ref, held_ref, out_ref, *refs):
    ring, core = place_ref[0], place_ref[1]
    b, size, count = ROWS_AT_ONCE, ROWS_AT_ONCE + 16, len(pieces)
    sems = refs[-1]
    if len(refs) > 1:
        held_basis_ref = refs[0]
        basis_copy = pltpu.make_async_copy(basis_ref, held_basis_ref, sems.at[2 * count])
        basis_copy.start()
    else:
        held_basis_ref = basis_ref
    copies = []
    for c in (1 - core, core):
        for s, h in pieces:
            i = len(copies)
            copies.append(
                pltpu.make_async_copy(
                    slab_ref.at[piece(ring, c, s, h)],
                    held_ref.at[i * b : (i + 1) * b],
                    sems.at[i],
                )
            )
            copies[-1].start()
    if len(refs) > 1:
        basis_copy.wait()
    for i in range(0, count, 2):
        for k in (i, i + 1):
            copies[k].wait()
        for k in (i, i + 1):
            x = jnp.dot(
                held_ref[k * b : (k + 1) * b, :],
                held_basis_ref[...],
                preferred_element_type=f32,
            )
            write_coded(out_ref.at[k * size : (k + 1) * size], x)
    for copy in copies[count:]:
        copy.wait()


def load_and_sketch(slab, basis, place, pieces, load_basis):
    d, k = basis.shape
    b, count = ROWS_AT_ONCE, len(pieces)
    vmem = pl.BlockSpec(memory_space=pltpu.VMEM)
    far = pl.BlockSpec(memory_space=pl.ANY)
    out_shape = [
        pltpu.VMEM((2 * count * b, d), slab.dtype),
        jax.ShapeDtypeStruct((count * (b + 16), k), f32),
    ]
    if load_basis:
        out_shape.append(pltpu.VMEM((d, k), basis.dtype))
    return pl.pallas_call(
        functools.partial(load_kernel, pieces),
        out_shape=out_shape,
        in_specs=[
            pl.BlockSpec(memory_space=pltpu.SMEM),
            far,
            far if load_basis else vmem,
        ],
        out_specs=[vmem] * len(out_shape),
        scratch_shapes=[pltpu.SemaphoreType.DMA((2 * count + 1,))],
        compiler_params=pltpu.CompilerParams(vmem_limit_bytes=VMEM_LIMIT),
        cost_estimate=pl.CostEstimate(
            flops=2 * count * b * d * k,
            bytes_accessed=count * b * (4 * d + 4 * k),
            transcendentals=0,
        ),
    )(
        place,
        pltpu.with_memory_space_constraint(slab, pltpu.HBM),
        pltpu.with_memory_space_constraint(basis, pltpu.HBM if load_basis else pltpu.VMEM),
    )


def sketch_kernel(slab_ref, basis_ref, other_ref, *outs):
    b, size, count = ROWS_AT_ONCE, ROWS_AT_ONCE + 16, len(outs)
    for i, out in enumerate(outs):
        x = jnp.dot(
            slab_ref[(count + i) * b : (count + i + 1) * b, :],
            basis_ref[...],
            preferred_element_type=f32,
        )
        x = x + read_coded(other_ref.at[i * size : (i + 1) * size])
        if out.shape[0] == b:
            out[...] = x
        else:
            write_coded(out, x)


def sketch_rows(held, basis, other, code):
    b, (d, k) = ROWS_AT_ONCE, basis.shape
    count = held.shape[0] // (2 * b)
    vmem = pl.BlockSpec(memory_space=pltpu.VMEM)
    return pl.pallas_call(
        sketch_kernel,
        out_shape=[jax.ShapeDtypeStruct((b + 16 if code else b, k), f32)] * count,
        in_specs=[vmem, vmem, vmem],
        out_specs=[vmem] * count,
        compiler_params=pltpu.CompilerParams(vmem_limit_bytes=VMEM_LIMIT),
        cost_estimate=pl.CostEstimate(
            flops=2 * count * b * d * k,
            bytes_accessed=count * b * (2 * d + 8 * k),
            transcendentals=0,
        ),
    )(
        pltpu.with_memory_space_constraint(held, pltpu.VMEM),
        pltpu.with_memory_space_constraint(basis, pltpu.VMEM),
        other,
    )


def add_kernel(a_ref, b_ref, c_ref, d_ref, up_ref, down_ref):
    write_coded(up_ref, a_ref[...] + read_coded(b_ref))
    write_coded(down_ref, c_ref[...] + read_coded(d_ref))


def add_received(a, b, c, d):
    vmem = pl.BlockSpec(memory_space=pltpu.VMEM)
    return pl.pallas_call(
        add_kernel,
        out_shape=(jax.ShapeDtypeStruct(b.shape, f32),) * 2,
        in_specs=[vmem] * 4,
        out_specs=(vmem, vmem),
        compiler_params=pltpu.CompilerParams(vmem_limit_bytes=VMEM_LIMIT),
        cost_estimate=pl.CostEstimate(
            flops=4 * a.size, bytes_accessed=24 * a.size, transcendentals=0
        ),
    )(a, b, c, d)


def gram_kernel(a_ref, b_ref, c_ref, d_ref, e_ref, f_ref, gram_ref, half_ref):
    n = gram_ref.shape[0]
    total = None
    for i, (own, first, second) in enumerate(
        ((a_ref, b_ref, c_ref), (d_ref, e_ref, f_ref))
    ):
        s = (own[...] + read_coded(first) + read_coded(second)).T
        top = s.astype(jnp.bfloat16)
        rest = (s - top.astype(f32)).astype(jnp.bfloat16)
        half_ref[i] = top
        both = jnp.concatenate([top, rest], axis=0)
        g = lax.dot_general(
            both, both, (((1,), (1,)), ((), ())), preferred_element_type=f32
        )
        g = (g[0:n, 0:n] + g[n:, n:]) + (g[0:n, n:] + g[n:, 0:n])
        total = g if total is None else total + g
    gram_ref[...] = total


def gram_and_half(low, high):
    rows, k = low[0].shape
    vmem = pl.BlockSpec(memory_space=pltpu.VMEM)
    return pl.pallas_call(
        gram_kernel,
        out_shape=(
            jax.ShapeDtypeStruct((k, k), f32),
            jax.ShapeDtypeStruct((2, k, rows), jnp.bfloat16),
        ),
        in_specs=[vmem] * 6,
        out_specs=(vmem, vmem),
        compiler_params=pltpu.CompilerParams(vmem_limit_bytes=VMEM_LIMIT),
        cost_estimate=pl.CostEstimate(
            flops=16 * rows * k * k, bytes_accessed=28 * rows * k, transcendentals=0
        ),
    )(*low, *high)


def factor_kernel(b, n, total_rows, place_ref, slab_ref, *refs):
    parts, halves, refs = refs[:2], refs[2:12], refs[12:]
    t_ref, p_ref, m_ref, y_ref, x_ref, sems = refs
    ring, core = place_ref[0], place_ref[1]
    sketch = []
    for c, (own, up, down, low, high) in ((core, halves[:5]), (1 - core, halves[5:])):
        for s, ref in ((0, own), (3, up), (1, down)):
            sketch += [(s, c, 0, ref.at[0]), (s, c, 1, ref.at[1])]
        sketch += [(2, c, 0, low), (2, c, 1, high)]
    count, rows = len(sketch), ROWS_AT_ONCE
    copies = []
    for i, (s, c, h, _) in enumerate(sketch):
        copies.append(
            pltpu.make_async_copy(slab_ref.at[piece(ring, c, s, h)], x_ref.at[i], sems.at[i])
        )
        copies[-1].start()
    size = n // 8
    for c, ref in zip((core, 1 - core), parts):
        for i in range(4):
            start = (c * 4 + (place_ref[2] + i) % 4) * size
            m_ref[pl.ds(pl.multiple_of(start, size), size), 0:n] = ref[
                i * size : (i + 1) * size, :
            ]
    ri = lax.broadcasted_iota(jnp.int32, (n, n), 0)
    ci = lax.broadcasted_iota(jnp.int32, (n, n), 1)
    m_ref[:, n : 2 * n] = jnp.where(ri == ci, 1.0, 0.0)
    steps = n // b
    for s in range(0, n, b):
        mine = range(s // b * count // steps, (s // b + 1) * count // steps)
        for i in mine:
            copies[i].wait()
        value = None if s == 0 else y_ref[...]
        for i in mine:
            term = jnp.dot(sketch[i][3][...], x_ref[i], preferred_element_type=f32)
            value = term if value is None else value + term
        y_ref[...] = value
        inverse = factor_diagonal(m_ref[s : s + b, s : s + b], b)
        lo, hi = s // 128 * 128, -(-(s + b) // 128) * 128
        rows_now = jnp.dot(
            inverse,
            m_ref[s : s + b, lo : n + hi],
            precision=HI,
            preferred_element_type=f32,
        )
        rr = lax.broadcasted_iota(jnp.int32, (b, n - lo), 0) + s
        cc = lax.broadcasted_iota(jnp.int32, (b, n - lo), 1) + lo
        left = jnp.where(cc >= rr, rows_now[:, 0 : n - lo], 0.0)
        right = rows_now[:, n - lo :]
        if lo:
            t_ref[s : s + b, 0:lo] = jnp.zeros((b, lo), f32)
        t_ref[s : s + b, lo:n] = left / jnp.sqrt(f32(total_rows))
        if s + b < n:
            start = (s + b) // 128 * 128
            left = left[:, start - lo :]
            update = lax.dot_general(
                left,
                jnp.concatenate([left, right], axis=1),
                (((0,), (0,)), ((), ())),
                precision=HI,
                preferred_element_type=f32,
            )
            m_ref[s + b : n, start : n + hi] = (
                m_ref[s + b : n, start : n + hi] - update[s + b - start :, :]
            )
        m_ref[s : s + b, n : n + hi] = right
    value = jnp.dot(
        m_ref[:, n : 2 * n], y_ref[...], precision=HI, preferred_element_type=f32
    )
    d = value.shape[1]
    value, e = coded(value)
    p_ref[:, 0:d] = value
    p_ref[:, d : d + 128] = jnp.broadcast_to(e, (n, 128))


def factor_and_project(gram, halves, slab, place, total_rows, b=64):
    n = gram[0].shape[1]
    rows, d = slab.shape
    count = rows // ROWS_AT_ONCE
    vmem = pl.BlockSpec(memory_space=pltpu.VMEM)
    return pl.pallas_call(
        functools.partial(factor_kernel, b, n, total_rows),
        out_shape=(
            jax.ShapeDtypeStruct((n, n), f32),
            jax.ShapeDtypeStruct((n, d + 128), f32),
        ),
        in_specs=[
            pl.BlockSpec(memory_space=pltpu.SMEM),
            pl.BlockSpec(memory_space=pl.ANY),
            *[vmem] * (len(gram) + len(halves)),
        ],
        out_specs=(vmem, vmem),
        scratch_shapes=[
            pltpu.VMEM((n, 2 * n), f32),
            pltpu.VMEM((n, d), f32),
            pltpu.VMEM((count, ROWS_AT_ONCE, d), slab.dtype),
            pltpu.SemaphoreType.DMA((count,)),
        ],
        compiler_params=pltpu.CompilerParams(vmem_limit_bytes=VMEM_LIMIT),
        cost_estimate=pl.CostEstimate(
            flops=12 * n**3 + 2 * rows * n * d,
            bytes_accessed=12 * n * n + 2 * rows * (n + d),
            transcendentals=n,
        ),
    )(place, pltpu.with_memory_space_constraint(slab, pltpu.HBM), *gram, *halves)


def shift_core(x):
    return lax.ppermute(x, "width", [(i, i ^ 1) for i in range(8)])


def shift_y(x, k):
    return lax.ppermute(x, "width", [(i, (i + 2 * k) % 8) for i in range(8)])


def shift_x(x, k):
    return lax.ppermute(
        x, "rows", [(i, i // 4 * 4 + (i % 4 + k) % 4) for i in range(32)]
    )


def shift_z(x, k):
    return lax.ppermute(x, "rows", [(i, (i + 4 * k) % 32) for i in range(32)])


def sum_of_four(x, shift, step=1):
    return (x + shift(x, 2 * step)) + (shift(x, step) + shift(x, -step))


def block_of(x, index, size):
    return lax.dynamic_slice_in_dim(x, index * size, size, 0)


def sum_everywhere(x, beside):
    core = lax.axis_index("width") % 2
    col = lax.axis_index("rows") % 4
    half, piece = x.shape[0] // 2, x.shape[0] // 8
    own = block_of(x, core, half) + shift_core(block_of(x, 1 - core, half))
    parts = [block_of(own, (col + k) % 4, piece) for k in range(4)]
    own = (parts[0] + shift_x(parts[2], 2)) + (
        shift_x(parts[1], 1) + shift_x(parts[3], -1)
    )
    own = sum_of_four(own, shift_z, 2)
    own, first = lax.optimization_barrier((own, beside(0, None)))
    own = own + lax.ppermute(own, "rows", [(i, i ^ 4) for i in range(32)])
    own = sum_of_four(own, shift_y)
    own, second = lax.optimization_barrier((own, beside(1, first)))
    ring = (own, shift_x(own, -1), shift_x(own, 2), shift_x(own, 1))
    own = jnp.concatenate(lax.optimization_barrier(ring), axis=0)
    return (own, shift_core(own)), first + second


def shards(slab, basis):
    width = lax.axis_index("width")
    total_rows = slab.shape[0] * lax.axis_size("rows")
    place = jnp.stack([width // 2, width % 2, lax.axis_index("rows") % 4]).astype(jnp.int32)

    held_first, first, held_basis = load_and_sketch(slab, basis, place, FIRST, True)
    first = shift_core(first.astype(f16))
    held_second, second = load_and_sketch(slab, held_basis, place, SECOND, False)
    first, second = lax.optimization_barrier((first, second))
    second = shift_core(second.astype(f16))
    far_up, far_down, near_up, near_down = sketch_rows(
        held_first, held_basis, first.astype(f32), True
    )
    far_up, far_down = shift_y(far_up.astype(f16), 1), shift_y(far_down.astype(f16), -1)
    near_up = shift_y(near_up.astype(f16), 1)
    near_down = shift_y(near_down.astype(f16), -1)
    up, down, low, high = sketch_rows(
        held_second, held_basis, second.astype(f32), False
    )

    up, down = add_received(up, far_up.astype(f32), down, far_down.astype(f32))
    up, down = shift_y(up.astype(f16), 1), shift_y(down.astype(f16), -1)
    gram, sketch = gram_and_half(
        (low, up.astype(f32), near_down.astype(f32)),
        (high, near_up.astype(f32), down.astype(f32)),
    )

    def gather(step, got):
        if step == 0:
            return (shift_y(sketch, 1), shift_y(sketch, -1))
        return (shift_y(got[0][0], 1), shift_y(got[1][1], -1))

    gram, others = sum_everywhere(gram, gather)
    halves = (sketch, *others)
    halves += tuple(shift_core(x) for x in halves)
    triangle, value = factor_and_project(gram, halves, slab, place, total_rows)
    pieces = lax.all_to_all(value.astype(f16), "rows", 0, 0, tiled=True).reshape(32, 8, -1)
    n = slab.shape[1]
    scale = jnp.exp2(pieces[:, :, n : n + 1].astype(f32) - 14.0)
    projected = jnp.sum(pieces[:, :, :n].astype(f32) * scale, axis=0).T
    return (projected, triangle)


def solution(mesh):
    return jax.shard_map(
        shards,
        mesh=mesh,
        in_specs=(P("rows", "width"), P("width", None)),
        out_specs=(P("width", "rows"), P()),
        check_vma=False,
    )
```

```python
import functools
import jax
import jax.numpy as jnp
from jax import lax
from jax.experimental import pallas as pl
from jax.experimental.pallas import tpu as pltpu
from jax.sharding import PartitionSpec as P

f32 = jnp.float32
f16 = jnp.float16
HI = lax.Precision.HIGHEST


def factor_diagonal(block, b, g=8):
    lane = lax.broadcasted_iota(jnp.int32, (b, 128), 1)
    row = lax.broadcasted_iota(jnp.int32, (b, 128), 0)
    a = jnp.concatenate([block, jnp.zeros((b, 128 - b), f32)], axis=1)
    a = jnp.where(lane == row + b, 1.0, a)
    sub = lax.broadcasted_iota(jnp.int32, (8, 128), 0)
    done = []
    for s in range(0, b, g):
        top, rest = a[0:g, :], a[g:, :]
        tiles = (b - s - g) // 8
        rows = [jnp.broadcast_to(top[k : k + 1, :], (8, 128)) for k in range(g)]
        u = {
            (k, m): jnp.broadcast_to(top[k : k + 1, s + m : s + m + 1], (8, 128))
            for k in range(g)
            for m in range(k, g)
        }
        cols = [
            [
                jnp.broadcast_to(rest[8 * t : 8 * t + 8, s + k : s + k + 1], (8, 128))
                for t in range(tiles)
            ]
            for k in range(g)
        ]
        for k in range(g):
            scale = lax.rsqrt(u[k, k])
            rows[k] = rows[k] * scale
            cols[k] = [c * scale for c in cols[k]]
            for m in range(k + 1, g):
                u[k, m] = u[k, m] * scale
            for m in range(k + 1, g):
                for q in range(m, g):
                    u[m, q] = u[m, q] - u[k, m] * u[k, q]
                rows[m] = rows[m] - u[k, m] * rows[k]
                cols[m] = [c - u[k, m] * d for c, d in zip(cols[m], cols[k])]
        final = rows[0]
        for k in range(1, g):
            final = jnp.where(sub == k, rows[k], final)
        done.append(final)
        if tiles:
            out = []
            for t in range(tiles):
                v = rest[8 * t : 8 * t + 8, :]
                for k in range(g):
                    v = v - cols[k][t] * rows[k]
                out.append(v)
            a = jnp.concatenate(out, axis=0)
    return jnp.concatenate(done, axis=0)[:, b : 2 * b]


ROWS_AT_ONCE = 512
VMEM_LIMIT = 24 << 20


def coded(x):
    e = jnp.ceil(jnp.log2(jnp.maximum(jnp.max(jnp.abs(x), keepdims=True), 1e-30)))
    return x * jnp.exp2(14.0 - e), e


def write_coded(out_ref, x):
    n = x.shape[0]
    y, e = coded(x)
    out_ref[0:n, :] = y
    out_ref[n : n + 16, :] = jnp.broadcast_to(e, (16, x.shape[1]))


def read_coded(ref):
    n = ref.shape[0] - 16
    return ref[0:n, :] * jnp.exp2(ref[n : n + 1, :] - 14.0)


FIRST = ((2, 0), (2, 1), (1, 1), (3, 0))
SECOND = ((1, 0), (3, 1), (0, 0), (0, 1))


def piece(ring, core, s, h):
    start = (((ring + s) % 4 * 2 + core) * 2 + h) * ROWS_AT_ONCE
    return pl.ds(pl.multiple_of(start, ROWS_AT_ONCE), ROWS_AT_ONCE)


def load_kernel(pieces, place_ref, slab_ref, basis_ref, held_ref, out_ref, *refs):
    ring, core = place_ref[0], place_ref[1]
    b, size, count = ROWS_AT_ONCE, ROWS_AT_ONCE + 16, len(pieces)
    sems = refs[-1]
    if len(refs) > 1:
        held_basis_ref = refs[0]
        basis_copy = pltpu.make_async_copy(basis_ref, held_basis_ref, sems.at[2 * count])
        basis_copy.start()
    else:
        held_basis_ref = basis_ref
    copies = []
    for c in (1 - core, core):
        for s, h in pieces:
            i = len(copies)
            copies.append(
                pltpu.make_async_copy(
                    slab_ref.at[piece(ring, c, s, h)],
                    held_ref.at[i * b : (i + 1) * b],
                    sems.at[i],
                )
            )
            copies[-1].start()
    if len(refs) > 1:
        basis_copy.wait()
    for i in range(0, count, 2):
        for k in (i, i + 1):
            copies[k].wait()
        for k in (i, i + 1):
            x = jnp.dot(
                held_ref[k * b : (k + 1) * b, :],
                held_basis_ref[...],
                preferred_element_type=f32,
            )
            write_coded(out_ref.at[k * size : (k + 1) * size], x)
    for copy in copies[count:]:
        copy.wait()


def load_and_sketch(slab, basis, place, pieces, load_basis):
    d, k = basis.shape
    b, count = ROWS_AT_ONCE, len(pieces)
    vmem = pl.BlockSpec(memory_space=pltpu.VMEM)
    far = pl.BlockSpec(memory_space=pl.ANY)
    out_shape = [
        pltpu.VMEM((2 * count * b, d), slab.dtype),
        jax.ShapeDtypeStruct((count * (b + 16), k), f32),
    ]
    if load_basis:
        out_shape.append(pltpu.VMEM((d, k), basis.dtype))
    return pl.pallas_call(
        functools.partial(load_kernel, pieces),
        out_shape=out_shape,
        in_specs=[
            pl.BlockSpec(memory_space=pltpu.SMEM),
            far,
            far if load_basis else vmem,
        ],
        out_specs=[vmem] * len(out_shape),
        scratch_shapes=[pltpu.SemaphoreType.DMA((2 * count + 1,))],
        compiler_params=pltpu.CompilerParams(vmem_limit_bytes=VMEM_LIMIT),
        cost_estimate=pl.CostEstimate(
            flops=2 * count * b * d * k,
            bytes_accessed=count * b * (4 * d + 4 * k),
            transcendentals=0,
        ),
    )(
        place,
        pltpu.with_memory_space_constraint(slab, pltpu.HBM),
        pltpu.with_memory_space_constraint(basis, pltpu.HBM if load_basis else pltpu.VMEM),
    )


def sketch_kernel(slab_ref, basis_ref, other_ref, *outs):
    b, size, count = ROWS_AT_ONCE, ROWS_AT_ONCE + 16, len(outs)
    for i, out in enumerate(outs):
        x = jnp.dot(
            slab_ref[(count + i) * b : (count + i + 1) * b, :],
            basis_ref[...],
            preferred_element_type=f32,
        )
        x = x + read_coded(other_ref.at[i * size : (i + 1) * size])
        if out.shape[0] == b:
            out[...] = x
        else:
            write_coded(out, x)


def sketch_rows(held, basis, other, code):
    b, (d, k) = ROWS_AT_ONCE, basis.shape
    count = held.shape[0] // (2 * b)
    vmem = pl.BlockSpec(memory_space=pltpu.VMEM)
    return pl.pallas_call(
        sketch_kernel,
        out_shape=[jax.ShapeDtypeStruct((b + 16 if code else b, k), f32)] * count,
        in_specs=[vmem, vmem, vmem],
        out_specs=[vmem] * count,
        compiler_params=pltpu.CompilerParams(vmem_limit_bytes=VMEM_LIMIT),
        cost_estimate=pl.CostEstimate(
            flops=2 * count * b * d * k,
            bytes_accessed=count * b * (2 * d + 8 * k),
            transcendentals=0,
        ),
    )(
        pltpu.with_memory_space_constraint(held, pltpu.VMEM),
        pltpu.with_memory_space_constraint(basis, pltpu.VMEM),
        other,
    )


def add_kernel(a_ref, b_ref, c_ref, d_ref, up_ref, down_ref):
    write_coded(up_ref, a_ref[...] + read_coded(b_ref))
    write_coded(down_ref, c_ref[...] + read_coded(d_ref))


def add_received(a, b, c, d):
    vmem = pl.BlockSpec(memory_space=pltpu.VMEM)
    return pl.pallas_call(
        add_kernel,
        out_shape=(jax.ShapeDtypeStruct(b.shape, f32),) * 2,
        in_specs=[vmem] * 4,
        out_specs=(vmem, vmem),
        compiler_params=pltpu.CompilerParams(vmem_limit_bytes=VMEM_LIMIT),
        cost_estimate=pl.CostEstimate(
            flops=4 * a.size, bytes_accessed=24 * a.size, transcendentals=0
        ),
    )(a, b, c, d)


def gram_kernel(a_ref, b_ref, c_ref, d_ref, e_ref, f_ref, gram_ref, half_ref):
    n = gram_ref.shape[0]
    total = None
    for i, (own, first, second) in enumerate(
        ((a_ref, b_ref, c_ref), (d_ref, e_ref, f_ref))
    ):
        s = (own[...] + read_coded(first) + read_coded(second)).T
        top = s.astype(jnp.bfloat16)
        rest = (s - top.astype(f32)).astype(jnp.bfloat16)
        half_ref[i] = top
        both = jnp.concatenate([top, rest], axis=0)
        g = lax.dot_general(
            both, both, (((1,), (1,)), ((), ())), preferred_element_type=f32
        )
        g = (g[0:n, 0:n] + g[n:, n:]) + (g[0:n, n:] + g[n:, 0:n])
        total = g if total is None else total + g
    gram_ref[...] = total


def gram_and_half(low, high):
    rows, k = low[0].shape
    vmem = pl.BlockSpec(memory_space=pltpu.VMEM)
    return pl.pallas_call(
        gram_kernel,
        out_shape=(
            jax.ShapeDtypeStruct((k, k), f32),
            jax.ShapeDtypeStruct((2, k, rows), jnp.bfloat16),
        ),
        in_specs=[vmem] * 6,
        out_specs=(vmem, vmem),
        compiler_params=pltpu.CompilerParams(vmem_limit_bytes=VMEM_LIMIT),
        cost_estimate=pl.CostEstimate(
            flops=16 * rows * k * k, bytes_accessed=28 * rows * k, transcendentals=0
        ),
    )(*low, *high)


def factor_kernel(b, n, total_rows, place_ref, slab_ref, *refs):
    parts, halves, refs = refs[:2], refs[2:12], refs[12:]
    t_ref, p_ref, m_ref, y_ref, x_ref, sems = refs
    ring, core = place_ref[0], place_ref[1]
    sketch = []
    for c, (own, up, down, low, high) in ((core, halves[:5]), (1 - core, halves[5:])):
        for s, ref in ((0, own), (3, up), (1, down)):
            sketch += [(s, c, 0, ref.at[0]), (s, c, 1, ref.at[1])]
        sketch += [(2, c, 0, low), (2, c, 1, high)]
    count, rows = len(sketch), ROWS_AT_ONCE
    copies = []
    for i, (s, c, h, _) in enumerate(sketch):
        copies.append(
            pltpu.make_async_copy(slab_ref.at[piece(ring, c, s, h)], x_ref.at[i], sems.at[i])
        )
        copies[-1].start()
    size = n // 8
    for c, ref in zip((core, 1 - core), parts):
        for i in range(4):
            start = (c * 4 + (place_ref[2] + i) % 4) * size
            m_ref[pl.ds(pl.multiple_of(start, size), size), 0:n] = ref[
                i * size : (i + 1) * size, :
            ]
    ri = lax.broadcasted_iota(jnp.int32, (n, n), 0)
    ci = lax.broadcasted_iota(jnp.int32, (n, n), 1)
    m_ref[:, n : 2 * n] = jnp.where(ri == ci, 1.0, 0.0)
    steps = n // b
    for s in range(0, n, b):
        mine = range(s // b * count // steps, (s // b + 1) * count // steps)
        for i in mine:
            copies[i].wait()
        value = None if s == 0 else y_ref[...]
        for i in mine:
            term = jnp.dot(sketch[i][3][...], x_ref[i], preferred_element_type=f32)
            value = term if value is None else value + term
        y_ref[...] = value
        inverse = factor_diagonal(m_ref[s : s + b, s : s + b], b)
        lo, hi = s // 128 * 128, -(-(s + b) // 128) * 128
        rows_now = jnp.dot(
            inverse,
            m_ref[s : s + b, lo : n + hi],
            precision=HI,
            preferred_element_type=f32,
        )
        rr = lax.broadcasted_iota(jnp.int32, (b, n - lo), 0) + s
        cc = lax.broadcasted_iota(jnp.int32, (b, n - lo), 1) + lo
        left = jnp.where(cc >= rr, rows_now[:, 0 : n - lo], 0.0)
        right = rows_now[:, n - lo :]
        if lo:
            t_ref[s : s + b, 0:lo] = jnp.zeros((b, lo), f32)
        t_ref[s : s + b, lo:n] = left / jnp.sqrt(f32(total_rows))
        if s + b < n:
            start = (s + b) // 128 * 128
            left = left[:, start - lo :]
            update = lax.dot_general(
                left,
                jnp.concatenate([left, right], axis=1),
                (((0,), (0,)), ((), ())),
                precision=HI,
                preferred_element_type=f32,
            )
            m_ref[s + b : n, start : n + hi] = (
                m_ref[s + b : n, start : n + hi] - update[s + b - start :, :]
            )
        m_ref[s : s + b, n : n + hi] = right
    value = jnp.dot(
        m_ref[:, n : 2 * n], y_ref[...], precision=HI, preferred_element_type=f32
    )
    d = value.shape[1]
    value, e = coded(value)
    p_ref[:, 0:d] = value
    p_ref[:, d : d + 128] = jnp.broadcast_to(e, (n, 128))


def factor_and_project(gram, halves, slab, place, total_rows, b=64):
    n = gram[0].shape[1]
    rows, d = slab.shape
    count = rows // ROWS_AT_ONCE
    vmem = pl.BlockSpec(memory_space=pltpu.VMEM)
    return pl.pallas_call(
        functools.partial(factor_kernel, b, n, total_rows),
        out_shape=(
            jax.ShapeDtypeStruct((n, n), f32),
            jax.ShapeDtypeStruct((n, d + 128), f32),
        ),
        in_specs=[
            pl.BlockSpec(memory_space=pltpu.SMEM),
            pl.BlockSpec(memory_space=pl.ANY),
            *[vmem] * (len(gram) + len(halves)),
        ],
        out_specs=(vmem, vmem),
        scratch_shapes=[
            pltpu.VMEM((n, 2 * n), f32),
            pltpu.VMEM((n, d), f32),
            pltpu.VMEM((count, ROWS_AT_ONCE, d), slab.dtype),
            pltpu.SemaphoreType.DMA((count,)),
        ],
        compiler_params=pltpu.CompilerParams(vmem_limit_bytes=VMEM_LIMIT),
        cost_estimate=pl.CostEstimate(
            flops=12 * n**3 + 2 * rows * n * d,
            bytes_accessed=12 * n * n + 2 * rows * (n + d),
            transcendentals=n,
        ),
    )(place, pltpu.with_memory_space_constraint(slab, pltpu.HBM), *gram, *halves)


def shift_core(x):
    return lax.ppermute(x, "width", [(i, i ^ 1) for i in range(8)])


def shift_y(x, k):
    return lax.ppermute(x, "width", [(i, (i + 2 * k) % 8) for i in range(8)])


def shift_x(x, k):
    return lax.ppermute(
        x, "rows", [(i, i // 4 * 4 + (i % 4 + k) % 4) for i in range(32)]
    )


def shift_z(x, k):
    return lax.ppermute(x, "rows", [(i, (i + 4 * k) % 32) for i in range(32)])


def sum_of_four(x, shift, step=1):
    far, up, down = lax.optimization_barrier(
        (shift(x, 2 * step), shift(x, step), shift(x, -step))
    )
    return (x + far) + (up + down)


def block_of(x, index, size):
    return lax.dynamic_slice_in_dim(x, index * size, size, 0)


def sum_everywhere(x, beside):
    core = lax.axis_index("width") % 2
    col = lax.axis_index("rows") % 4
    half, piece = x.shape[0] // 2, x.shape[0] // 8
    own = block_of(x, core, half) + shift_core(block_of(x, 1 - core, half))
    parts = [block_of(own, (col + k) % 4, piece) for k in range(4)]
    own = (parts[0] + shift_x(parts[2], 2)) + (
        shift_x(parts[1], 1) + shift_x(parts[3], -1)
    )
    own = sum_of_four(own, shift_z, 2)
    own, first = lax.optimization_barrier((own, beside(0, None)))
    own = own + lax.ppermute(own, "rows", [(i, i ^ 4) for i in range(32)])
    own = sum_of_four(own, shift_y)
    own, second = lax.optimization_barrier((own, beside(1, first)))
    ring = (own, shift_x(own, -1), shift_x(own, 2), shift_x(own, 1))
    own = jnp.concatenate(lax.optimization_barrier(ring), axis=0)
    return (own, shift_core(own)), first + second


def shards(slab, basis):
    width = lax.axis_index("width")
    total_rows = slab.shape[0] * lax.axis_size("rows")
    place = jnp.stack([width // 2, width % 2, lax.axis_index("rows") % 4]).astype(jnp.int32)

    held_first, first, held_basis = load_and_sketch(slab, basis, place, FIRST, True)
    first = shift_core(first.astype(f16))
    held_second, second = load_and_sketch(slab, held_basis, place, SECOND, False)
    first, second = lax.optimization_barrier((first, second))
    second = shift_core(second.astype(f16))
    far_up, far_down, near_up, near_down = sketch_rows(
        held_first, held_basis, first.astype(f32), True
    )
    far_up, far_down = shift_y(far_up.astype(f16), 1), shift_y(far_down.astype(f16), -1)
    near_up = shift_y(near_up.astype(f16), 1)
    near_down = shift_y(near_down.astype(f16), -1)
    up, down, low, high = sketch_rows(
        held_second, held_basis, second.astype(f32), False
    )

    up, down = add_received(up, far_up.astype(f32), down, far_down.astype(f32))
    up, down = shift_y(up.astype(f16), 1), shift_y(down.astype(f16), -1)
    gram, sketch = gram_and_half(
        (low, up.astype(f32), near_down.astype(f32)),
        (high, near_up.astype(f32), down.astype(f32)),
    )

    def gather(step, got):
        if step == 0:
            return (shift_y(sketch, 1), shift_y(sketch, -1))
        return (shift_y(got[0][0], 1), shift_y(got[1][1], -1))

    gram, others = sum_everywhere(gram, gather)
    halves = (sketch, *others)
    halves += tuple(shift_core(x) for x in halves)
    triangle, value = factor_and_project(gram, halves, slab, place, total_rows)
    pieces = lax.all_to_all(value.astype(f16), "rows", 0, 0, tiled=True).reshape(32, 8, -1)
    n = slab.shape[1]
    scale = jnp.exp2(pieces[:, :, n : n + 1].astype(f32) - 14.0)
    projected = jnp.sum(pieces[:, :, :n].astype(f32) * scale, axis=0).T
    return (projected, triangle)


def solution(mesh):
    return jax.shard_map(
        shards,
        mesh=mesh,
        in_specs=(P("rows", "width"), P("width", None)),
        out_specs=(P("width", "rows"), P()),
        check_vma=False,
    )
```
